32 devices in a mesh: dp: 2 (over y), expert: 16 (over z, x, core).
Axes of the slice: x: 2, y: 2, z: 4, core: 2. Of those that a mesh axis runs over, the one named last changes fastest.
Arguments:
- tokens: bfloat16 [1024, 2048], P(('dp', 'expert')), may hold values from -6 to 6
- routes: int32 [1024, 8], P(('dp', 'expert')), may hold values from 0 to 15, all different within a row; in each aligned block of 32 rows (0 to 31, 32 to 63, ...) at most 24 rows name the same one
- gates: float32 [1024, 8], P(('dp', 'expert')), may hold values from 0.1 to 0.6
- w_gate: bfloat16 [16, 2048, 768], P('expert'), may hold values from -0.125 to 0.125
- w_up: bfloat16 [16, 2048, 768], P('expert'), may hold values from -0.125 to 0.125
- w_down: bfloat16 [16, 768, 2048], P('expert'), may hold values from -0.21875 to 0.21875
- swap_flags: int32 [16], replicated, may hold values from 0 to 1, as said below
- d_out: bfloat16 [1024, 2048], P(('dp', 'expert')), may hold values from -6 to 6
Outputs:
- mixture: bfloat16 [1024, 2048], P(('dp', 'expert'))
- d_tokens: bfloat16 [1024, 2048], P(('dp', 'expert'))
- d_gates: float32 [1024, 8], P(('dp', 'expert'))
- g_gate: bfloat16 [16, 2048, 768], P('expert', 'dp')
- g_up: bfloat16 [16, 2048, 768], P('expert', 'dp')
- g_down: bfloat16 [16, 768, 2048], P('expert', None, 'dp')
The draws below stay inside these ranges and needn't reach their ends.
Inputs may be any that keep to these rules, and one draw needn't show every extreme that they name: `routes`: among the 32 rows of one device no expert is named more than 24 times, and in every draw some device names some expert exactly 24 times. swap_flags[i] equals swap_flags[i + 8]; swap_flags[0] and swap_flags[7] are 1.
All inputs are finite; a program needn't handle non-finite values.
Results may differ from the reference program's by a relative error of at most 0.0095.
Values may be sent and summed in bfloat16 or wider, within the bound.
A program may use at most 128 MiB of HBM per device.

```python
import math
import jax
import jax.numpy as jnp
import numpy as np
from jax import lax

D = 2048
FF = 768
TOPK = 8
TOK_DEV = 32
EXPERTS = 16
CAP = 24
TOKENS = 1024
N_DP = 2
N_EXPERT = 16


def draw_swap_flags(key, part):
    pair_bits = jax.random.randint(key, (EXPERTS // 2,), 0, 2).astype(jnp.int32)
    pair_bits = pair_bits.at[0].set(1).at[EXPERTS // 2 - 1].set(1)
    return jnp.concatenate([pair_bits, pair_bits])


def level_of(own_key, extent, split, low, top_value):
    def one(dim, shards_of):
        heights = jax.random.uniform(jax.random.fold_in(jax.random.fold_in(own_key, 6), dim), (shards_of,), jnp.float32, low / len(split), top_value / len(split))
        return jnp.repeat(jnp.exp(heights), extent[dim] // shards_of).reshape((-1,) + (1,) * (len(extent) - dim - 1))

    level = one(*split[0])
    for cut in split[1:]:
        level = level * one(*cut)
    return level


def deal_out(rng, own, number, rows, amount, top, most, skew):
    ranking = jax.random.permutation(rng, amount)
    crowded, common = load_shares(amount, rows * top, most, skew, True), load_shares(amount, rows * top, most, skew, False)
    places = jnp.arange(amount)

    def named(tallies, rotation):
        used = int((tallies > 0).sum())
        fixed = max(1, used // 4)
        passed = fixed + (places - fixed + rotation * (used - fixed)) % max(1, amount - fixed)
        return jnp.zeros((amount,), jnp.int32).at[ranking[jnp.where(places < fixed, places, passed)]].set(jnp.asarray(tallies, jnp.int32))

    tallies = jnp.where(number % 4 == 0, named(crowded, number // 4), named(common, number - number // 4 - 1))
    mixed = jax.random.permutation(jax.random.fold_in(own, 3), amount)
    giver, taker = mixed[0:amount // 2 * 2:2], mixed[1:amount // 2 * 2:2]
    room = jnp.minimum(tallies[giver] - 1, most - tallies[taker]) // 2
    room = jnp.where((giver == ranking[0]) | (taker == ranking[0]) | (tallies[taker] == 0), 0, jnp.maximum(room, 0))
    passed = jax.random.randint(jax.random.fold_in(own, 4), (amount // 2,), 0, 1 << 20) % (room + 1)
    tallies = tallies.at[giver].add(-passed).at[taker].add(passed)
    labels = jnp.searchsorted(jnp.cumsum(tallies), jnp.arange(rows * top), side="right").astype(jnp.int32)
    listing = labels.reshape(top, rows).T
    listing = listing[jax.random.permutation(jax.random.fold_in(own, 1), rows)]
    rotation = jax.random.randint(jax.random.fold_in(own, 2), (rows, 1), 0, top)
    return jnp.take_along_axis(listing, (jnp.arange(top)[None, :] + rotation) % top, axis=1)


def load_shares(count, total, limit, slope, full):
    weights = [(1 << 20) // math.isqrt(standing ** slope) + 1 for standing in range(1, count + 1)]
    largest = limit if full else min(limit, max(-(-total // count), total * weights[0] // sum(weights)))
    least = 1 if total - largest >= count - 1 else 0
    counts, spare = [largest] + [least] * (count - 1), total - largest - least * (count - 1)
    while spare > 0:
        movable = [i for i in range(1, count) if counts[i] < largest] or [i for i in range(1, count) if counts[i] < limit]
        mass, left = sum([weights[i] for i in movable]), spare
        for i in movable:
            addition = min(limit - counts[i], max(1, left * weights[i] // mass), spare)
            counts[i] = counts[i] + addition
            spare = spare - addition
    return np.array(counts)


def normal_values(stream_key, dims, scale, bound, shards=(), kind=jnp.bfloat16):
    level = level_of(stream_key, dims, shards, -0.22, 0.18) if shards else 1.0
    values = jax.random.normal(stream_key, dims, jnp.float32) * scale * level
    return jnp.minimum(jnp.maximum(values, -bound), bound).astype(kind)


def setup_inputs(seed: int = 0) -> dict:
    arg_keys = jax.random.split(jax.random.key(seed), 9)
    tokens = normal_values(arg_keys[0], (TOKENS, D), 1.0, 6.0, ((0, 32),))
    routes_keys = jax.random.split(jax.random.fold_in(arg_keys[1], 1), TOKENS // TOK_DEV)
    routes_turns = jax.random.permutation(jax.random.fold_in(arg_keys[1], 3), TOKENS // TOK_DEV)
    routes = jax.vmap(lambda own, number: deal_out(jax.random.fold_in(arg_keys[1], 2), own, number, TOK_DEV, EXPERTS, TOPK, CAP, 2))(routes_keys, routes_turns).reshape((TOKENS, TOPK))
    gates = jnp.clip(0.1 + 0.5 * jax.random.uniform(arg_keys[2], (TOKENS, TOPK), jnp.float32) ** level_of(arg_keys[2], (TOKENS, TOPK), ((0, 32),), -0.2, 0.2), 0.1, 0.6)
    w_gate = normal_values(arg_keys[3], (EXPERTS, D, FF), D ** -0.5, 0.125, ((0, 16),))
    w_up = normal_values(arg_keys[4], (EXPERTS, D, FF), D ** -0.5, 0.125, ((0, 16),))
    w_down = normal_values(arg_keys[5], (EXPERTS, FF, D), FF ** -0.5, 0.21875, ((0, 16),))
    swap_flags = draw_swap_flags(jax.random.fold_in(arg_keys[8], 71), 0)
    d_out = normal_values(arg_keys[7], (TOKENS, D), 1.0, 6.0, ((0, 32),))
    return {"tokens": tokens, "routes": routes, "gates": gates, "w_gate": w_gate, "w_up": w_up, "w_down": w_down, "swap_flags": swap_flags, "d_out": d_out}


def expert_pass(inputs):
    w_gate_one, w_up_one, w_down_one, slot_token, slot_pair, slot_alive, token_table, expert_cot = inputs
    gate_f = w_gate_one.astype(jnp.float32)
    up_f = w_up_one.astype(jnp.float32)
    down_f = w_down_one.astype(jnp.float32)
    rows_in = token_table[slot_token].astype(jnp.float32) * slot_alive[:, None]
    cot_rows = expert_cot[slot_pair].astype(jnp.float32) * slot_alive[:, None]
    pre_gate = jnp.dot(rows_in, gate_f)
    pre_up = jnp.dot(rows_in, up_f)
    logistic = jax.nn.sigmoid(pre_gate)
    activated = pre_gate * logistic
    hidden = (activated * pre_up).astype(jnp.bfloat16)
    expert_out = jnp.dot(hidden.astype(jnp.float32), down_f).astype(jnp.bfloat16)
    d_hidden = jnp.dot(cot_rows, down_f.T)
    grad_gate_pre = (d_hidden * pre_up * logistic * (1.0 + pre_gate * (1.0 - logistic))).astype(jnp.bfloat16)
    grad_up_pre = (d_hidden * activated).astype(jnp.bfloat16)
    d_part = (jnp.dot(grad_gate_pre.astype(jnp.float32), gate_f.T) + jnp.dot(grad_up_pre.astype(jnp.float32), up_f.T)).astype(jnp.bfloat16)
    rows_grp = rows_in.reshape(N_DP, -1, D)
    gate_grp = grad_gate_pre.astype(jnp.float32).reshape(N_DP, -1, FF)
    up_grp = grad_up_pre.astype(jnp.float32).reshape(N_DP, -1, FF)
    hid_grp = hidden.astype(jnp.float32).reshape(N_DP, -1, FF)
    cot_grp = cot_rows.reshape(N_DP, -1, D)

    def reduce_rows(partial_value):
        rounded = lax.optimization_barrier(partial_value.astype(jnp.bfloat16))
        return jnp.sum(rounded.astype(jnp.float32), axis=0).astype(jnp.bfloat16)

    grad_gate = reduce_rows(jnp.einsum('rnd,rnf->rdf', rows_grp, gate_grp))
    grad_up = reduce_rows(jnp.einsum('rnd,rnf->rdf', rows_grp, up_grp))
    grad_down = reduce_rows(jnp.einsum('rnf,rnd->rfd', hid_grp, cot_grp))
    return expert_out, d_part, grad_gate, grad_up, grad_down


def reference(tokens, routes, gates, w_gate, w_up, w_down, swap_flags, d_out):
    devices = N_DP * N_EXPERT
    per_device = TOK_DEV * TOPK
    route_flat = routes.reshape(devices, per_device)
    onehot = (route_flat[:, :, None] == jnp.arange(EXPERTS, dtype=jnp.int32)[None, None, :]).astype(jnp.int32)
    before = jnp.cumsum(onehot, axis=1) - onehot
    position = jnp.sum(onehot * before, axis=2)
    source = jnp.arange(devices, dtype=jnp.int32)[:, None]
    slot_index = ((route_flat * devices + source) * CAP + position).reshape(-1).astype(jnp.int32)
    total_slots = EXPERTS * devices * CAP
    pair_ids = jnp.arange(TOKENS * TOPK, dtype=jnp.int32)
    slot_token = jnp.zeros((total_slots,), jnp.int32).at[slot_index].set(pair_ids // TOPK)
    slot_pair = jnp.zeros((total_slots,), jnp.int32).at[slot_index].set(pair_ids)
    slot_alive = jnp.zeros((total_slots,), jnp.float32).at[slot_index].set(1.0)
    expert_cot = (gates[:, :, None] * d_out.astype(jnp.float32)[:, None, :]).astype(jnp.bfloat16).reshape(TOKENS * TOPK, D)

    def one_expert(inputs):
        return expert_pass(inputs + (tokens, expert_cot))

    outs_all, parts_all, grad_gate, grad_up, grad_down = lax.map(one_expert, (w_gate, w_up, w_down, slot_token.reshape(EXPERTS, -1), slot_pair.reshape(EXPERTS, -1), slot_alive.reshape(EXPERTS, -1)))
    expert_out = outs_all.reshape(-1, D)[slot_index].reshape(TOKENS, TOPK, D)
    d_part = parts_all.reshape(-1, D)[slot_index].reshape(TOKENS, TOPK, D)
    mixture = jnp.sum(gates[:, :, None] * expert_out.astype(jnp.float32), axis=1).astype(jnp.bfloat16)
    d_gates = jnp.einsum('td,tkd->tk', d_out.astype(jnp.float32), expert_out.astype(jnp.float32))
    d_tokens = jnp.sum(d_part.astype(jnp.float32), axis=1).astype(jnp.bfloat16)
    slots = jnp.arange(EXPERTS, dtype=jnp.int32)
    half_axis = EXPERTS // 2
    partner = jnp.where(slots < half_axis, slots + half_axis, slots - half_axis)
    placed = jnp.where(swap_flags == 1, partner, slots).astype(jnp.int32)
    return mixture, d_tokens, d_gates, grad_gate[placed], grad_up[placed], grad_down[placed]
```

```python
import jax
import jax.numpy as jnp
from jax import lax
from jax.sharding import PartitionSpec as P

F32 = jnp.float32
BF16 = jnp.bfloat16


def dot(left, right, lhs_dim, rhs_dim):
    return lax.dot_general(
        left, right, (((lhs_dim,), (rhs_dim,)), ((), ())), preferred_element_type=F32
    )


def row_picker(column, capacity):
    count = column.shape[0]
    routed = column > 0
    earlier = jnp.arange(count)[:, None] < jnp.arange(count)[None, :]
    position = dot(routed.astype(BF16)[None], earlier.astype(BF16), 1, 0).astype(jnp.int32)
    picks = (position == jnp.arange(capacity, dtype=jnp.int32)[:, None]) & routed[None]
    weight = jnp.sum(jnp.where(picks, column[None], 0.0), axis=1, keepdims=True)
    return picks.astype(BF16), weight


def on_device(tokens, routes, gates, w_gate, w_up, w_down, swap_flags, d_out):
    experts = lax.axis_size("expert")
    groups = lax.axis_size("dp")
    own = lax.axis_index("expert")
    group = lax.axis_index("dp")
    tok_count, width = tokens.shape
    top = routes.shape[1]
    ff = w_gate.shape[2]
    part = width // groups
    rows = experts * tok_count
    capacity = experts * min(
        tok_count, (3 * tok_count * top + 2 * experts - 1) // (2 * experts)
    )
    gate_mat, up_mat, down_mat = w_gate[0], w_up[0], w_down[0]
    swapped = swap_flags[own] == 1
    ids = jnp.arange(experts, dtype=jnp.int32)

    dense = jnp.sum(
        jnp.where(routes[:, :, None] == ids, gates[:, :, None], 0.0), axis=1
    )
    dense_all = lax.all_gather(dense, ("dp", "expert"), tiled=True)
    both = lax.all_gather(
        jnp.concatenate([tokens, d_out], axis=1), "expert", tiled=True
    )

    def column_of(who, expert):
        block = lax.dynamic_slice_in_dim(dense_all, who * rows, rows, 0)
        return jnp.sum(jnp.where(ids == expert, block, 0.0), axis=1)

    picks, weight = row_picker(column_of(group, own), capacity)
    picked = dot(picks, both, 1, 0).astype(BF16)
    x, cot = picked[:, :width], picked[:, width:]

    pre_gate = dot(x, gate_mat, 1, 0)
    pre_up = dot(x, up_mat, 1, 0)
    logistic = jax.nn.sigmoid(pre_gate)
    activated = pre_gate * logistic
    hidden = (activated * pre_up).astype(BF16)
    d_expert = (weight * cot.astype(F32)).astype(BF16)
    d_hidden = dot(d_expert, down_mat, 1, 1)
    d_gate_pre = (
        d_hidden * pre_up * logistic * (1.0 + pre_gate * (1.0 - logistic))
    ).astype(BF16)
    d_up_pre = (d_hidden * activated).astype(BF16)

    half = experts // 2
    trade = [(i, (i + half) % experts) for i in range(experts)]

    def place(mine):
        return jnp.where(swapped, lax.ppermute(mine, "expert", trade), mine)

    acts = (place(hidden), place(jnp.concatenate([d_gate_pre, d_up_pre], axis=1)))

    result = dot(hidden, down_mat, 1, 0).astype(BF16)
    result_f = result.astype(F32)
    mixed = (weight * result_f).astype(BF16)
    mixture = lax.psum_scatter(
        dot(picks, mixed, 0, 0).astype(BF16), "expert", scatter_dimension=0, tiled=True
    )
    d_rows = (dot(d_gate_pre, gate_mat, 1, 1) + dot(d_up_pre, up_mat, 1, 1)).astype(BF16)
    d_tokens = lax.psum_scatter(
        dot(picks, d_rows, 0, 0).astype(BF16), "expert", scatter_dimension=0, tiled=True
    )
    inner = jnp.sum(result_f * cot.astype(F32), axis=1, keepdims=True)
    inner = jnp.sum(picks.astype(F32) * inner, axis=0).reshape(experts, tok_count)
    inner = lax.all_to_all(inner, "expert", split_axis=0, concat_axis=0, tiled=True)
    d_gates = jnp.sum(
        jnp.where(routes[:, :, None] == ids, inner.T[:, None, :], 0.0), axis=2
    )

    placed = jnp.where(swapped, (own + half) % experts, own)
    split = both.reshape(rows, 2, groups, part)
    xs, cots, hiddens, pres = [], [], [], []
    for shift in range(groups):
        target = (group + shift) % groups
        source = (group + groups - shift) % groups
        block = lax.dynamic_index_in_dim(split, target, 2, keepdims=False)
        block = block.reshape(rows, 2 * part)
        h, pre = acts
        if shift:
            ring = [(i, (i + shift) % groups) for i in range(groups)]
            block = lax.ppermute(block, "dp", ring)
            h = lax.ppermute(h, "dp", ring)
            pre = lax.ppermute(pre, "dp", ring)
        choose, scale = row_picker(column_of(source, placed), capacity)
        chosen = dot(choose, block, 1, 0).astype(BF16)
        xs.append(chosen[:, :part])
        cots.append((scale * chosen[:, part:].astype(F32)).astype(BF16))
        hiddens.append(h)
        pres.append(pre)
    g_pre = dot(jnp.concatenate(xs), jnp.concatenate(pres), 0, 0).astype(BF16)
    g_down = dot(jnp.concatenate(hiddens), jnp.concatenate(cots), 0, 0).astype(BF16)
    return (mixture, d_tokens, d_gates, g_pre[None, :, :ff], g_pre[None, :, ff:], g_down[None])


def solution(mesh):
    rows = P(("dp", "expert"), None)
    mats = P("expert", None, None)
    return jax.shard_map(
        on_device,
        mesh=mesh,
        in_specs=(rows, rows, rows, mats, mats, mats, P(), rows),
        out_specs=(rows, rows, rows, P("expert", "dp", None), P("expert", "dp", None), P("expert", None, "dp")),
        check_vma=False,
    )
```

```python
import jax
import jax.numpy as jnp
from jax import lax
from jax.sharding import PartitionSpec as P

F32 = jnp.float32
BF16 = jnp.bfloat16


def dot(left, right, lhs_dim, rhs_dim):
    return lax.dot_general(
        left, right, (((lhs_dim,), (rhs_dim,)), ((), ())), preferred_element_type=F32
    )


def row_picker(column, capacity):
    count = column.shape[0]
    routed = column > 0
    earlier = jnp.arange(count)[:, None] < jnp.arange(count)[None, :]
    position = dot(routed.astype(BF16)[None], earlier.astype(BF16), 1, 0).astype(jnp.int32)
    picks = (position == jnp.arange(capacity, dtype=jnp.int32)[:, None]) & routed[None]
    weight = jnp.sum(jnp.where(picks, column[None], 0.0), axis=1, keepdims=True)
    return picks.astype(BF16), weight


def bit_of(index, bit):
    return (index // (1 << bit)) % 2


def swap_bit(value, bit):
    size = lax.axis_size("expert")
    return lax.ppermute(value, "expert", [(i, i ^ (1 << bit)) for i in range(size)])


def gather_rows(block, order):
    own = lax.axis_index("expert")
    held, done = block, []
    for bit in order:
        other = swap_bit(held, bit)
        at = sum(b > bit for b in done)
        high = bit_of(own, bit) == 1
        held = jnp.stack(
            [jnp.where(high, other, held), jnp.where(high, held, other)], axis=at
        )
        done.append(bit)
    return held.reshape(-1, block.shape[-1])


def scatter_sum(partial, bits):
    own = lax.axis_index("expert")
    size, width = partial.shape[0] >> bits, partial.shape[1]
    for bit in range(bits):
        pairs = partial.reshape(-1, 2, size, width)
        high = bit_of(own, bit) == 1
        keep = jnp.where(high, pairs[:, 1], pairs[:, 0])
        give = jnp.where(high, pairs[:, 0], pairs[:, 1])
        partial = (keep.astype(F32) + swap_bit(give, bit).astype(F32)).astype(BF16)
    return partial.reshape(size, width)


def after(value, *others):
    return lax.optimization_barrier((value, *others))[0]


def terms_of(value):
    terms = []
    for _ in range(3):
        term = lax.reduce_precision(value, 8, 7)
        terms.append(term.astype(BF16))
        value = value - term
    return terms


def on_device(tokens, routes, gates, w_gate, w_up, w_down, swap_flags, d_out):
    experts = lax.axis_size("expert")
    groups = lax.axis_size("dp")
    own = lax.axis_index("expert")
    group = lax.axis_index("dp")
    tok_count, width = tokens.shape
    top = routes.shape[1]
    ff = w_gate.shape[2]
    part = width // groups
    rows = experts * tok_count
    capacity = experts * min(
        tok_count, (3 * tok_count * top + 2 * experts - 1) // (2 * experts)
    )
    gate_mat, up_mat, down_mat = w_gate[0], w_up[0], w_down[0]
    swapped = swap_flags[own] == 1
    ids = jnp.arange(experts, dtype=jnp.int32)

    dense = jnp.sum(
        jnp.where(routes[:, :, None] == ids, gates[:, :, None], 0.0), axis=1
    )
    bits = experts.bit_length() - 1
    spare = jnp.zeros((tok_count, -3 * experts % 128), BF16)
    first = gather_rows(
        jnp.concatenate([tokens, *terms_of(dense), spare], axis=1), range(bits - 1, -1, -1)
    )
    d_out_all = gather_rows(d_out, [*range(1, bits), 0])
    tokens_all, table = first[:, :width], first[:, width:]

    def column_of(table, expert):
        terms = table[:, : 3 * experts].astype(F32).reshape(rows, 3, experts)
        block = terms[:, 0] + (terms[:, 1] + terms[:, 2])
        return jnp.sum(jnp.where(ids == expert, block, 0.0), axis=1)

    picks, weight = row_picker(column_of(table, own), capacity)
    x = dot(picks, tokens_all, 1, 0).astype(BF16)
    cot = dot(picks, d_out_all, 1, 0).astype(BF16)

    pre_gate = dot(x, gate_mat, 1, 0)
    pre_up = dot(x, up_mat, 1, 0)
    logistic = jax.nn.sigmoid(pre_gate)
    activated = pre_gate * logistic
    hidden = (activated * pre_up).astype(BF16)
    d_expert = (weight * cot.astype(F32)).astype(BF16)
    d_hidden = dot(d_expert, down_mat, 1, 1)
    d_gate_pre = (
        d_hidden * pre_up * logistic * (1.0 + pre_gate * (1.0 - logistic))
    ).astype(BF16)
    d_up_pre = (d_hidden * activated).astype(BF16)

    half = experts // 2
    trade = [(i, (i + half) % experts) for i in range(experts)]

    pres = jnp.concatenate([d_gate_pre, d_up_pre], axis=1)
    far_hidden = lax.ppermute(hidden, "expert", trade)
    far_pres = lax.ppermute(pres, "expert", trade)

    result = dot(hidden, down_mat, 1, 0).astype(BF16)
    result_f = result.astype(F32)
    mixed = (weight * result_f).astype(BF16)
    mixture = scatter_sum(dot(picks, mixed, 0, 0).astype(BF16), bits)
    d_rows = (dot(d_gate_pre, gate_mat, 1, 1) + dot(d_up_pre, up_mat, 1, 1)).astype(BF16)
    d_tokens = scatter_sum(dot(picks, d_rows, 0, 0).astype(BF16), bits)
    inner = jnp.sum(result_f * cot.astype(F32), axis=1, keepdims=True)
    inner = jnp.sum(picks.astype(F32) * inner, axis=0).reshape(experts, tok_count)
    inner = lax.all_to_all(inner, "expert", split_axis=0, concat_axis=0, tiled=True)
    d_gates = jnp.sum(
        jnp.where(routes[:, :, None] == ids, inner.T[:, None, :], 0.0), axis=2
    )

    placed = jnp.where(swapped, (own + half) % experts, own)
    acts = (
        jnp.where(swapped, after(far_hidden, mixture), hidden),
        jnp.where(swapped, after(far_pres, d_tokens), pres),
    )
    xs, cots, hiddens, pre_parts = [], [], [], []
    for shift in range(groups):
        target = (group + shift) % groups
        block = jnp.concatenate(
            [lax.dynamic_slice_in_dim(a, target * part, part, 1) for a in (tokens_all, d_out_all)]
            + [table],
            axis=1,
        )
        h, pre = acts
        if shift:
            ring = [(i, (i + shift) % groups) for i in range(groups)]
            block = lax.ppermute(block, "dp", ring)
            h = lax.ppermute(h, "dp", ring)
            pre = lax.ppermute(pre, "dp", ring)
        choose, scale = row_picker(column_of(block[:, 2 * part :], placed), capacity)
        chosen = dot(choose, block[:, : 2 * part], 1, 0).astype(BF16)
        xs.append(chosen[:, :part])
        cots.append((scale * chosen[:, part:].astype(F32)).astype(BF16))
        hiddens.append(h)
        pre_parts.append(pre)
    g_pre = dot(jnp.concatenate(xs), jnp.concatenate(pre_parts), 0, 0).astype(BF16)
    g_down = dot(jnp.concatenate(hiddens), jnp.concatenate(cots), 0, 0).astype(BF16)
    return (mixture, d_tokens, d_gates, g_pre[None, :, :ff], g_pre[None, :, ff:], g_down[None])


def solution(mesh):
    rows = P(("dp", "expert"), None)
    mats = P("expert", None, None)
    return jax.shard_map(
        on_device,
        mesh=mesh,
        in_specs=(rows, rows, rows, mats, mats, mats, P(), rows),
        out_specs=(rows, rows, rows, P("expert", "dp", None), P("expert", "dp", None), P("expert", None, "dp")),
        check_vma=False,
    )
```

```python
import jax
import jax.numpy as jnp
from jax import lax
from jax.sharding import PartitionSpec as P

F32 = jnp.float32
BF16 = jnp.bfloat16


def dot(left, right, lhs_dim, rhs_dim):
    return lax.dot_general(
        left, right, (((lhs_dim,), (rhs_dim,)), ((), ())), preferred_element_type=F32
    )


def row_picker(column, capacity):
    count = column.shape[0]
    routed = column > 0
    earlier = jnp.arange(count)[:, None] < jnp.arange(count)[None, :]
    position = dot(routed.astype(BF16)[None], earlier.astype(BF16), 1, 0).astype(jnp.int32)
    picks = (position == jnp.arange(capacity, dtype=jnp.int32)[:, None]) & routed[None]
    weight = jnp.sum(jnp.where(picks, column[None], 0.0), axis=1, keepdims=True)
    return picks.astype(BF16), weight


def bit_of(index, bit):
    return (index // (1 << bit)) % 2


def swap_bit(value, bit):
    size = lax.axis_size("expert")
    return lax.ppermute(value, "expert", [(i, i ^ (1 << bit)) for i in range(size)])


def gather_rows(block, order):
    own = lax.axis_index("expert")
    held, done = block, []
    for bit in order:
        other = swap_bit(held, bit)
        at = sum(b > bit for b in done)
        high = bit_of(own, bit) == 1
        held = jnp.stack(
            [jnp.where(high, other, held), jnp.where(high, held, other)], axis=at
        )
        done.append(bit)
    return held.reshape(-1, block.shape[-1])


def scatter_sum(partial, bits):
    own = lax.axis_index("expert")
    size, width = partial.shape[0] >> bits, partial.shape[1]
    for bit in range(bits):
        pairs = partial.reshape(-1, 2, size, width)
        high = bit_of(own, bit) == 1
        keep = jnp.where(high, pairs[:, 1], pairs[:, 0])
        give = jnp.where(high, pairs[:, 0], pairs[:, 1])
        partial = (keep.astype(F32) + swap_bit(give, bit).astype(F32)).astype(BF16)
    return partial.reshape(size, width)


def after(value, *others):
    return lax.optimization_barrier((value, *others))[0]


def terms_of(value):
    terms = []
    for _ in range(3):
        term = lax.reduce_precision(value, 8, 7)
        terms.append(term.astype(BF16))
        value = value - term
    return terms


def on_device(tokens, routes, gates, w_gate, w_up, w_down, swap_flags, d_out):
    experts = lax.axis_size("expert")
    groups = lax.axis_size("dp")
    own = lax.axis_index("expert")
    group = lax.axis_index("dp")
    tok_count, width = tokens.shape
    top = routes.shape[1]
    part = width // groups
    rows = experts * tok_count
    capacity = experts * min(
        tok_count, (3 * tok_count * top + 2 * experts - 1) // (2 * experts)
    )
    gate_mat, up_mat, down_mat = w_gate[0], w_up[0], w_down[0]
    swapped = swap_flags[own] == 1
    ids = jnp.arange(experts, dtype=jnp.int32)

    dense = jnp.sum(
        jnp.where(routes[:, :, None] == ids, gates[:, :, None], 0.0), axis=1
    )
    bits = experts.bit_length() - 1
    spare = jnp.zeros((tok_count, -3 * experts % 128), BF16)
    first = gather_rows(
        jnp.concatenate([tokens, *terms_of(dense), spare], axis=1), range(bits - 1, -1, -1)
    )
    d_out_all = gather_rows(d_out, [*range(1, bits), 0])
    tokens_all, table = first[:, :width], first[:, width:]

    def column_of(table, expert):
        terms = table[:, : 3 * experts].astype(F32).reshape(rows, 3, experts)
        block = terms[:, 0] + (terms[:, 1] + terms[:, 2])
        return jnp.sum(jnp.where(ids == expert, block, 0.0), axis=1)

    picks, weight = row_picker(column_of(table, own), capacity)
    x = dot(picks, tokens_all, 1, 0).astype(BF16)
    cot = dot(picks, d_out_all, 1, 0).astype(BF16)

    pre_gate = dot(x, gate_mat, 1, 0)
    pre_up = dot(x, up_mat, 1, 0)
    logistic = jax.nn.sigmoid(pre_gate)
    activated = pre_gate * logistic
    hidden = (activated * pre_up).astype(BF16)
    d_expert = (weight * cot.astype(F32)).astype(BF16)
    d_hidden = dot(d_expert, down_mat, 1, 1)
    d_gate_pre = (
        d_hidden * pre_up * logistic * (1.0 + pre_gate * (1.0 - logistic))
    ).astype(BF16)
    d_up_pre = (d_hidden * activated).astype(BF16)

    half = experts // 2
    trade = [(i, (i + half) % experts) for i in range(experts)]

    far_hidden = lax.ppermute(hidden, "expert", trade)
    far_gate = lax.ppermute(d_gate_pre, "expert", trade)
    far_up = lax.ppermute(d_up_pre, "expert", trade)

    result = dot(after(hidden, d_gate_pre, d_up_pre), down_mat, 1, 0).astype(BF16)
    result_f = result.astype(F32)
    mixed = (weight * result_f).astype(BF16)
    mixture = scatter_sum(dot(picks, mixed, 0, 0).astype(BF16), bits)
    d_rows = (dot(d_gate_pre, gate_mat, 1, 1) + dot(d_up_pre, up_mat, 1, 1)).astype(BF16)
    d_spread = dot(picks, d_rows, 0, 0).astype(BF16)
    d_tokens = scatter_sum(d_spread, bits)
    result_f = after(result, d_tokens).astype(F32)
    inner = jnp.sum(result_f * cot.astype(F32), axis=1, keepdims=True)
    inner = jnp.sum(picks.astype(F32) * inner, axis=0).reshape(experts, tok_count)
    inner = lax.all_to_all(inner, "expert", split_axis=0, concat_axis=0, tiled=True)
    d_gates = jnp.sum(
        jnp.where(routes[:, :, None] == ids, inner.T[:, None, :], 0.0), axis=2
    )

    placed = jnp.where(swapped, (own + half) % experts, own)
    acts = (
        jnp.where(swapped, after(far_hidden, d_spread), hidden),
        jnp.where(swapped, after(far_gate, mixture), d_gate_pre),
        jnp.where(swapped, after(far_up, d_tokens), d_up_pre),
    )
    late_tokens, late_d_out, late_table = lax.optimization_barrier(
        (tokens_all, d_out_all, table, d_gate_pre, d_up_pre)
    )[:3]
    xs, cots, acts_of = [], [], []
    for shift in range(groups):
        target = (group + shift) % groups
        block = jnp.concatenate(
            [lax.dynamic_slice_in_dim(a, target * part, part, 1) for a in (late_tokens, late_d_out)]
            + [late_table],
            axis=1,
        )
        parts = acts
        if shift:
            ring = [(i, (i + shift) % groups) for i in range(groups)]
            block = after(lax.ppermute(block, "dp", ring), mixture)
            parts = [lax.ppermute(a, "dp", ring) for a in acts]
        choose, scale = row_picker(column_of(block[:, 2 * part :], placed), capacity)
        chosen = dot(choose, block[:, : 2 * part], 1, 0).astype(BF16)
        xs.append(chosen[:, :part])
        cots.append((scale * chosen[:, part:].astype(F32)).astype(BF16))
        acts_of.append(parts)
    x, cot = jnp.concatenate(xs), jnp.concatenate(cots)
    hidden, d_gate_pre, d_up_pre = (jnp.concatenate(a) for a in zip(*acts_of))
    g_down = dot(hidden, cot, 0, 0).astype(BF16)
    g_gate = dot(x, d_gate_pre, 0, 0).astype(BF16)
    g_up = dot(x, d_up_pre, 0, 0).astype(BF16)
    return (mixture, d_tokens, d_gates, g_gate[None], g_up[None], g_down[None])


def solution(mesh):
    rows = P(("dp", "expert"), None)
    mats = P("expert", None, None)
    return jax.shard_map(
        on_device,
        mesh=mesh,
        in_specs=(rows, rows, rows, mats, mats, mats, P(), rows),
        out_specs=(rows, rows, rows, P("expert", "dp", None), P("expert", "dp", None), P("expert", None, "dp")),
        check_vma=False,
    )
```

```python
import jax
import jax.numpy as jnp
from jax import lax
from jax.sharding import PartitionSpec as P

F32 = jnp.float32
BF16 = jnp.bfloat16


def dot(left, right, lhs_dim, rhs_dim):
    return lax.dot_general(
        left, right, (((lhs_dim,), (rhs_dim,)), ((), ())), preferred_element_type=F32
    )


def row_picker(column, capacity):
    count = column.shape[0]
    routed = column > 0
    earlier = jnp.arange(count)[:, None] < jnp.arange(count)[None, :]
    position = dot(routed.astype(BF16)[None], earlier.astype(BF16), 1, 0).astype(jnp.int32)
    picks = (position == jnp.arange(capacity, dtype=jnp.int32)[:, None]) & routed[None]
    weight = jnp.sum(jnp.where(picks, column[None], 0.0), axis=1, keepdims=True)
    return picks.astype(BF16), weight


def bit_of(index, bit):
    return (index // (1 << bit)) % 2


def swap_bit(value, bit):
    size = lax.axis_size("expert")
    return lax.ppermute(value, "expert", [(i, i ^ (1 << bit)) for i in range(size)])


def gather_rows(block, order):
    own = lax.axis_index("expert")
    held, done = block, []
    for bit in order:
        other = swap_bit(held, bit)
        at = sum(b > bit for b in done)
        high = bit_of(own, bit) == 1
        held = jnp.stack(
            [jnp.where(high, other, held), jnp.where(high, held, other)], axis=at
        )
        done.append(bit)
    return held.reshape(-1, block.shape[-1])


def scatter_sum(partial, bits):
    own = lax.axis_index("expert")
    size, width = partial.shape[0] >> bits, partial.shape[1]
    for bit in range(bits):
        pairs = partial.reshape(-1, 2, size, width)
        high = bit_of(own, bit) == 1
        keep = jnp.where(high, pairs[:, 1], pairs[:, 0])
        give = jnp.where(high, pairs[:, 0], pairs[:, 1])
        partial = (keep.astype(F32) + swap_bit(give, bit).astype(F32)).astype(BF16)
    return partial.reshape(size, width)


def after(value, *others):
    return lax.optimization_barrier((value, *others))[0]


def terms_of(value):
    terms = []
    for _ in range(3):
        term = lax.reduce_precision(value, 8, 7)
        terms.append(term.astype(BF16))
        value = value - term
    return terms


def on_device(tokens, routes, gates, w_gate, w_up, w_down, swap_flags, d_out):
    experts = lax.axis_size("expert")
    groups = lax.axis_size("dp")
    own = lax.axis_index("expert")
    group = lax.axis_index("dp")
    tok_count, width = tokens.shape
    top = routes.shape[1]
    part = width // groups
    rows = experts * tok_count
    capacity = experts * min(
        tok_count, (3 * tok_count * top + 2 * experts - 1) // (2 * experts)
    )
    gate_mat, up_mat, down_mat = w_gate[0], w_up[0], w_down[0]
    swapped = swap_flags[own] == 1
    ids = jnp.arange(experts, dtype=jnp.int32)

    dense = jnp.sum(
        jnp.where(routes[:, :, None] == ids, gates[:, :, None], 0.0), axis=1
    )
    bits = experts.bit_length() - 1
    spare = jnp.zeros((tok_count, -3 * experts % 128), BF16)
    first = gather_rows(
        jnp.concatenate([tokens, *terms_of(dense), spare], axis=1), range(bits - 1, -1, -1)
    )
    d_out_all = gather_rows(d_out, [*range(1, bits), 0])
    tokens_all, table = first[:, :width], first[:, width:]

    def column_of(table, expert):
        terms = table[:, : 3 * experts].astype(F32).reshape(rows, 3, experts)
        block = terms[:, 0] + (terms[:, 1] + terms[:, 2])
        return jnp.sum(jnp.where(ids == expert, block, 0.0), axis=1)

    picks, weight = row_picker(column_of(table, own), capacity)
    x = dot(picks, tokens_all, 1, 0).astype(BF16)
    cot = dot(picks, d_out_all, 1, 0).astype(BF16)

    pre_gate = dot(x, gate_mat, 1, 0)
    pre_up = dot(x, up_mat, 1, 0)
    logistic = jax.nn.sigmoid(pre_gate)
    activated = pre_gate * logistic
    hidden = (activated * pre_up).astype(BF16)
    d_expert = (weight * cot.astype(F32)).astype(BF16)
    d_hidden = dot(d_expert, down_mat, 1, 1)
    d_gate_pre = (
        d_hidden * pre_up * logistic * (1.0 + pre_gate * (1.0 - logistic))
    ).astype(BF16)
    d_up_pre = (d_hidden * activated).astype(BF16)

    half = experts // 2
    trade = [(i, (i + half) % experts) for i in range(experts)]

    far_hidden = lax.ppermute(hidden, "expert", trade)
    pres = jnp.concatenate([d_gate_pre, d_up_pre], axis=1)
    far_pres = lax.ppermute(pres, "expert", trade)

    result = dot(after(hidden, d_gate_pre, d_up_pre), down_mat, 1, 0).astype(BF16)
    result_f = result.astype(F32)
    mixed = (weight * result_f).astype(BF16)
    mixture = scatter_sum(dot(picks, mixed, 0, 0).astype(BF16), bits)
    d_rows = (dot(d_gate_pre, gate_mat, 1, 1) + dot(d_up_pre, up_mat, 1, 1)).astype(BF16)
    d_spread = dot(picks, d_rows, 0, 0).astype(BF16)
    d_tokens = scatter_sum(d_spread, bits)
    result_f = after(result, d_tokens).astype(F32)
    inner = jnp.sum(result_f * cot.astype(F32), axis=1, keepdims=True)
    inner = jnp.sum(picks.astype(F32) * inner, axis=0).reshape(experts, tok_count)
    inner = lax.all_to_all(inner, "expert", split_axis=0, concat_axis=0, tiled=True)
    d_gates = jnp.sum(
        jnp.where(routes[:, :, None] == ids, inner.T[:, None, :], 0.0), axis=2
    )

    placed = jnp.where(swapped, (own + half) % experts, own)
    acts = (
        jnp.where(swapped, after(far_hidden, mixture, d_tokens), hidden),
        jnp.where(swapped, after(far_pres, mixture, d_tokens), pres),
    )
    late_tokens, late_d_out, late_table = lax.optimization_barrier(
        (tokens_all, d_out_all, table, d_gate_pre, d_up_pre)
    )[:3]
    xs, cots, acts_of = [], [], []
    for shift in range(groups):
        target = (group + shift) % groups
        block = jnp.concatenate(
            [lax.dynamic_slice_in_dim(a, target * part, part, 1) for a in (late_tokens, late_d_out)]
            + [late_table],
            axis=1,
        )
        parts = acts
        if shift:
            ring = [(i, (i + shift) % groups) for i in range(groups)]
            block = after(lax.ppermute(block, "dp", ring), mixture, d_tokens)
            parts = [lax.ppermute(a, "dp", ring) for a in acts]
        choose, scale = row_picker(column_of(block[:, 2 * part :], placed), capacity)
        chosen = dot(choose, block[:, : 2 * part], 1, 0).astype(BF16)
        xs.append(chosen[:, :part])
        cots.append((scale * chosen[:, part:].astype(F32)).astype(BF16))
        acts_of.append(parts)
    x, cot = jnp.concatenate(xs), jnp.concatenate(cots)
    hidden, pres = (jnp.concatenate(a) for a in zip(*acts_of))
    g_down = dot(hidden, cot, 0, 0).astype(BF16)
    g_pre = dot(x, pres, 0, 0).astype(BF16)
    ff = hidden.shape[1]
    return (mixture, d_tokens, d_gates, g_pre[None, :, :ff], g_pre[None, :, ff:], g_down[None])


def solution(mesh):
    rows = P(("dp", "expert"), None)
    mats = P("expert", None, None)
    return jax.shard_map(
        on_device,
        mesh=mesh,
        in_specs=(rows, rows, rows, mats, mats, mats, P(), rows),
        out_specs=(rows, rows, rows, P("expert", "dp", None), P("expert", "dp", None), P("expert", None, "dp")),
        check_vma=False,
    )
```
